512 devices in a mesh: head: 8 (over y, core), seq: 64 (over x, z).
Axes of the slice: x: 4, y: 4, z: 16, core: 2. Of those that a mesh axis runs over, the one named last changes fastest.
Arguments:
- keys: bfloat16 [1048576, 128], P(('head', 'seq')), parts along dimension 0, may hold values from -6 to 6
- values: bfloat16 [1048576, 128], P(('head', 'seq')), parts along dimension 0, may hold values from -6 to 6
- queries: bfloat16 [1048576, 128], P(('head', 'seq')), parts along dimension 0, may hold values from -160 to 160
- query_positions: int32 [4096], P(('head', 'seq')), parts along dimension 0, may hold values from 0 to 131071, as said below
- kept_index: int32 [4096], P('head'), parts along dimension 0, may hold values from 0 to 131071, as said below
- ridge_level: int32 [8], P('head'), parts along dimension 0, may hold values from 20 to 99
Outputs:
- matched_values: float32 [4096, 128], P('head'), parts along dimension 0
- ref_out: float32 [4096, 128], P(('head', 'seq')), parts along dimension 0
The draws below stay inside these ranges and needn't reach their ends.
There are 8 independent parts, one for each index of `head`. The reference program is written for one: setup_inputs(seed, part) draws one part's arguments, and reference() takes and returns one part's arrays. A program takes and returns all parts, laid end to end along the dimension named above; each array names one. Nothing has to cross between parts.
Inputs may be any that keep to these rules, and one draw needn't show every extreme that they name: `query_positions`: entries 8 d to 8 (d + 1) - 1 are distinct increasing positions within the slab of positions 2048 d to 2048 (d + 1) - 1. `kept_index`: distinct and increasing.
All inputs are finite; a program needn't handle non-finite values.
Results may differ from the reference program's by a relative error of at most 0.00051.
Values may be sent and summed in bfloat16 or wider, within the bound.
No kernel may reach another device: no remote copies, remote signals or barrier semaphores. Data moves between devices by JAX's collectives and lax.ppermute only.
A program may use at most 64 MiB of HBM per device.

```python
import math
import jax
import jax.numpy as jnp
from jax import lax

HD = 128
TOK_DEV = 2048
Q_DEV = 8
KEEP = 512
CACHE = 131072
N_SEQ = 64


def shared_integers(key):
    slab_keys = jax.random.split(jax.random.fold_in(key, 101), N_SEQ)

    def slab_rows(slab_key, slab_number):
        chosen = jax.random.permutation(slab_key, TOK_DEV)[:Q_DEV]
        return jnp.sort(chosen).astype(jnp.int32) + slab_number * TOK_DEV
    slab_numbers = jnp.arange(N_SEQ, dtype=jnp.int32)
    positions = jax.vmap(slab_rows)(slab_keys, slab_numbers).reshape(-1).astype(jnp.int32)
    everyone = jax.random.permutation(jax.random.fold_in(key, 102), TOK_DEV * N_SEQ)
    kept = jnp.sort(everyone[:KEEP]).astype(jnp.int32)
    return (positions, kept)


def shared_floats(key):
    total = TOK_DEV * N_SEQ
    base_keys = jnp.clip(jax.random.normal(jax.random.fold_in(key, 103), (total, HD), jnp.float32), -6.0, 6.0)
    base_queries = jnp.clip(3.0 * jax.random.normal(jax.random.fold_in(key, 104), (total, HD), jnp.float32), -18.0, 18.0)
    return (base_keys, base_queries)


def draw_keys(key, part):
    return shared_floats(key)[0].astype(jnp.bfloat16)


def draw_queries(key, part):
    return shared_floats(key)[1].astype(jnp.bfloat16)


def draw_query_positions(key, part):
    return shared_integers(key)[0]


def draw_kept_index(key, part):
    return shared_integers(key)[1]


def level_of(rng, shape, pieces, least, largest):
    def one(dim, shards_of):
        draws = jax.random.uniform(jax.random.fold_in(jax.random.fold_in(rng, 6), dim), (shards_of,), jnp.float32, least / len(pieces), largest / len(pieces))
        return jnp.repeat(jnp.exp(draws), shape[dim] // shards_of).reshape((-1,) + (1,) * (len(shape) - dim - 1))

    level = one(*pieces[0])
    for cut in pieces[1:]:
        level = level * one(*cut)
    return level


def normal_values(stream_key, extent, width, limit, shards=(), held_as=jnp.bfloat16):
    drawn = width * jax.random.normal(stream_key, extent, jnp.float32)
    if shards:
        drawn = drawn * level_of(stream_key, extent, shards, -0.22, 0.18)
    return jnp.clip(drawn, -limit, limit).astype(held_as)


def setup_inputs(seed: int = 0, part: int = 0) -> dict:
    key_list = jax.random.split(jax.random.key(seed), 7)
    part_keys = jax.random.split(jax.random.fold_in(key_list[6], part), 7)
    keys = draw_keys(jax.random.fold_in(jax.random.fold_in(key_list[6], part), 71), part)
    values = normal_values(part_keys[1], (CACHE, HD), 1.0, 6.0, ((0, 64),))
    queries = draw_queries(jax.random.fold_in(jax.random.fold_in(key_list[6], part), 71), part)
    query_positions = draw_query_positions(jax.random.fold_in(jax.random.fold_in(key_list[6], part), 71), part)
    kept_index = draw_kept_index(jax.random.fold_in(jax.random.fold_in(key_list[6], part), 71), part)
    ridge_level = jax.random.randint(part_keys[5], (1,), 20, 100).astype(jnp.int32)
    return dict(keys=keys, values=values, queries=queries, query_positions=query_positions, kept_index=kept_index, ridge_level=ridge_level)


def slab_partials(query_rows, key_slab, value_slab):
    inv_root = 1.0 / math.sqrt(HD)
    scores = jnp.dot(query_rows.astype(jnp.float32), key_slab.T.astype(jnp.float32), preferred_element_type=jnp.float32) * inv_root
    row_peak = lax.optimization_barrier(jnp.max(scores, axis=1))
    probs = jnp.exp(scores - row_peak[:, None]).astype(jnp.bfloat16)
    totals = lax.optimization_barrier(jnp.sum(probs.astype(jnp.float32), axis=1))
    numer = jnp.dot(probs.astype(jnp.float32), value_slab.astype(jnp.float32), preferred_element_type=jnp.float32)
    return (row_peak, totals, numer)

def reference(keys, values, queries, query_positions, kept_index, ridge_level):
    inv_root = 1.0 / math.sqrt(HD)
    query_rows = jnp.take(queries, query_positions.astype(jnp.int32), axis=0)
    kept_keys = jnp.take(keys, kept_index.astype(jnp.int32), axis=0)
    key_slabs = keys.reshape(N_SEQ, TOK_DEV, HD)
    value_slabs = values.reshape(N_SEQ, TOK_DEV, HD)

    def one_slab(pair):
        return slab_partials(query_rows, pair[0], pair[1])
    maxima, totals, numers = lax.map(one_slab, (key_slabs, value_slabs))
    overall = lax.optimization_barrier(jnp.max(maxima, axis=0))
    factors = jnp.exp(maxima - overall[None, :])
    ref_out = lax.optimization_barrier(jnp.sum(numers * factors[:, :, None], axis=0)) / lax.optimization_barrier(jnp.sum(totals * factors, axis=0))[:, None]
    logits = jnp.dot(query_rows.astype(jnp.float32), kept_keys.T.astype(jnp.float32), preferred_element_type=jnp.float32) * inv_root
    weights = jax.nn.softmax(logits, axis=1)
    gram = jnp.dot(weights.T, weights, precision=lax.Precision.HIGHEST)
    moment = jnp.dot(weights.T, ref_out, precision=lax.Precision.HIGHEST)
    ridge_value = ridge_level[0].astype(jnp.float32) * 0.01
    system = gram + ridge_value * jnp.eye(KEEP, dtype=jnp.float32)
    lower = jnp.linalg.cholesky(system)
    matched_values = jax.scipy.linalg.cho_solve((lower, True), moment)
    return (matched_values, ref_out)
```

```python
import math

import jax
import jax.numpy as jnp
from jax import lax
from jax.experimental import pallas as pl
from jax.experimental.pallas import tpu as pltpu
from jax.sharding import PartitionSpec as P

SEQ = "seq"
FULL = 32767.0
FINE = 65536.0
LOWEST = -28


def swap(blocks):
    return lax.all_to_all(blocks, SEQ, 0, 0, tiled=True)


def power_of_two(k):
    low = jnp.left_shift(jnp.int32(1), jnp.clip(k + 30, 0, 30)).astype(jnp.float32)
    high = jnp.left_shift(jnp.int32(1), jnp.clip(k, 0, 30)).astype(jnp.float32)
    deep = jnp.left_shift(jnp.int32(1), jnp.clip(k + 60, 0, 30)).astype(jnp.float32)
    return low * (2.0**-30) * high * deep * (2.0**-30)


def code_of(x):
    x = x.astype(jnp.float32)
    size = jnp.abs(x)
    step = jnp.zeros(x.shape, jnp.int32)
    unit = jnp.full(x.shape, 2.0 ** (7 - LOWEST), jnp.float32)
    for e in range(LOWEST + 1, 3):
        reached = size >= 2.0**e
        step = jnp.where(reached, e - LOWEST, step)
        unit = jnp.where(reached, 2.0 ** (7 - e), unit)
    digits = (size * unit).astype(jnp.int32)
    code = jnp.where(size >= 2.0**LOWEST, step * 128 + digits, 0)
    return jnp.where(x < 0, -code, code).astype(jnp.int16)


def decoded(code):
    code = code.astype(jnp.int32)
    size = jnp.maximum(jnp.abs(code) - 128, 0)
    step = size >> 7
    digits = jnp.where(code == 0, 0, (size & 127) + 128)
    value = digits.astype(jnp.float32) * jnp.left_shift(jnp.int32(1), step).astype(jnp.float32)
    value = value * 2.0 ** (LOWEST - 7)
    return jnp.where(code < 0, -value, value).astype(jnp.bfloat16)


def in_two(x):
    high = x.astype(jnp.bfloat16)
    return high, (x - high.astype(jnp.float32)).astype(jnp.bfloat16)


def product(a, b, dims):
    def one(u, v):
        return lax.dot_general(u, v, (dims, ((), ())), preferred_element_type=jnp.float32)

    return one(a[0], b[0]) + (one(a[0], b[1]) + one(a[1], b[0]))


ROWS = ((1,), (0,))
BY_ROW = ((0,), (0,))
BY_COLUMN = ((1,), (1,))


def solve_kernel(level_ref, queries_ref, kept_ref, out_ref, system_ref, weights_ref, inverse_ref, rest_ref):
    size = system_ref.shape[0]
    inv_root = 1.0 / math.sqrt(queries_ref.shape[1])
    logits = lax.dot_general(
        queries_ref[...], kept_ref[...], (BY_COLUMN, ((), ())), preferred_element_type=jnp.float32
    ) * inv_root
    weights = jnp.exp(logits - jnp.max(logits, axis=1, keepdims=True))
    weights = weights / jnp.sum(weights, axis=1, keepdims=True)
    weights_ref[...] = weights
    parts = in_two(weights)
    gram = product(parts, parts, BY_ROW)
    ridge = level_ref[0].astype(jnp.float32) * 0.01
    bound = jnp.max(jnp.sum(weights, axis=0, keepdims=True), axis=1, keepdims=True) * 1.0001
    row = lax.broadcasted_iota(jnp.int32, (size, size), 0)
    column = lax.broadcasted_iota(jnp.int32, (size, size), 1)
    eye = jnp.where(row == column, 1.0, 0.0)
    system = gram + ridge * eye
    system_ref[...] = system
    span = jnp.max(bound) + 2.0 * ridge
    first = 2.0 / span
    rest = eye - first * system
    rest_ref[...] = rest
    inverse_ref[...] = first * eye
    reach = span / jnp.max(bound)

    def step(reach):
        ahead = 2.0 * reach * reach
        scale = ahead / (ahead - 1.0)
        rest = in_two(rest_ref[...])
        inverse = inverse_ref[...]
        inverse_ref[...] = scale * (inverse + product(in_two(inverse), rest, ROWS))
        rest_ref[...] = scale * product(rest, rest, ROWS) - (scale - 1.0) * eye
        return ahead - 1.0

    lax.while_loop(lambda reach: reach < 4096.0, step, reach)
    inverse = inverse_ref[...]
    rest = eye - jnp.dot(
        system_ref[...], inverse, precision=lax.Precision.HIGHEST, preferred_element_type=jnp.float32
    )
    inverse = inverse + product(in_two(inverse), in_two(rest), ROWS)
    out_ref[...] = product(in_two(inverse), in_two(weights_ref[...]), BY_COLUMN)


def solve_rows(level, queries, kept):
    count, size = queries.shape[0], kept.shape[0]
    vmem = pl.BlockSpec(memory_space=pltpu.VMEM)
    return pl.pallas_call(
        solve_kernel,
        out_shape=jax.ShapeDtypeStruct((size, count), jnp.float32),
        in_specs=[pl.BlockSpec(memory_space=pltpu.SMEM), vmem, vmem],
        out_specs=vmem,
        scratch_shapes=[
            pltpu.VMEM((size, size), jnp.float32),
            pltpu.VMEM((count, size), jnp.float32),
            pltpu.VMEM((size, size), jnp.float32),
            pltpu.VMEM((size, size), jnp.float32),
        ],
        compiler_params=pltpu.CompilerParams(vmem_limit_bytes=40 * 2**20),
        cost_estimate=pl.CostEstimate(flops=12 * 10**9, bytes_accessed=2 * 2**20, transcendentals=2**18),
        name="solve",
    )(level, queries, kept)


def per_device(keys, values, queries, query_positions, kept_index, ridge_level):
    slab_len, head_dim = keys.shape
    own_count = query_positions.shape[0]
    peers = lax.axis_size(SEQ)
    own_kept = kept_index.shape[0] // peers
    inv_root = 1.0 / math.sqrt(head_dim)
    slab_start = lax.axis_index(SEQ) * slab_len
    own_queries = jnp.take(queries, query_positions - slab_start, axis=0)
    offset = kept_index - slab_start
    inside = (offset >= 0) & (offset < slab_len)
    picked = jnp.where(
        inside[:, None], jnp.take(keys, jnp.clip(offset, 0, slab_len - 1), axis=0), 0
    ).astype(jnp.bfloat16)
    sent = jnp.concatenate(
        [
            jnp.broadcast_to(own_queries[None], (peers, own_count, head_dim)),
            picked.reshape(peers, own_kept, head_dim),
        ],
        axis=1,
    )
    got = swap(sent)
    all_queries = got[:, :own_count].reshape(peers * own_count, head_dim)
    kept_block = jnp.sum(got[:, own_count:].astype(jnp.float32), axis=0)

    scores = jnp.dot(all_queries, keys.T, preferred_element_type=jnp.float32) * inv_root
    peak = jnp.max(scores, axis=1)
    probs = jnp.exp(scores - peak[:, None]).astype(jnp.bfloat16)
    total = jnp.sum(probs.astype(jnp.float32), axis=1)
    numer = jnp.dot(probs, values, preferred_element_type=jnp.float32)

    mean = numer / total[:, None]
    most = jnp.max(jnp.abs(mean), axis=1)
    power = jnp.clip(jnp.ceil(jnp.log2(jnp.maximum(most, 2.0**-58))), -58, 3).astype(jnp.int32)
    spread = mean / power_of_two(power)[:, None]
    coarse = jnp.clip(jnp.round(spread * FULL), -FULL, FULL).astype(jnp.int16)

    def in_words(x):
        whole = jnp.floor(x)
        fine = jnp.minimum(jnp.round((x - whole) * FINE), FINE - 1.0) - FINE / 2
        return whole, fine

    peak_whole, peak_fine = in_words(peak)
    sent_peak = peak_whole + (peak_fine + FINE / 2) / FINE
    share_whole, share_fine = in_words(jnp.log(total) + (peak - sent_peak))
    marks = jnp.stack([peak_whole, peak_fine, share_whole, share_fine, power.astype(jnp.float32)], axis=-1)
    marks = jnp.pad(marks, ((0, 0), (0, head_dim - marks.shape[1]))).astype(jnp.int16)
    sent = jnp.concatenate(
        [
            coarse.reshape(peers, own_count, head_dim),
            jnp.broadcast_to(code_of(kept_block)[None], (peers, own_kept, head_dim)),
            marks.reshape(peers, own_count, head_dim),
        ],
        axis=1,
    )
    got = swap(sent)
    kept_keys = decoded(got[:, own_count : own_count + own_kept]).reshape(peers * own_kept, head_dim)
    marks = got[:, own_count + own_kept :].astype(jnp.float32)
    peaks = marks[:, :, 0] + (marks[:, :, 1] + FINE / 2) / FINE
    shares = marks[:, :, 2] + (marks[:, :, 3] + FINE / 2) / FINE
    factors = jnp.exp(peaks - jnp.max(peaks, axis=0)[None] + shares)
    scales = factors * power_of_two(marks[:, :, 4].astype(jnp.int32)) / FULL
    means = got[:, :own_count].astype(jnp.float32)
    ref_out = jnp.sum(means * scales[:, :, None], axis=0) / jnp.sum(factors, axis=0)[:, None]

    whole = swap(jnp.broadcast_to(ref_out[None], (peers, own_count, head_dim)))
    rows = solve_rows(ridge_level, all_queries, kept_keys)
    whole = whole.reshape(peers * own_count, head_dim)
    matched_values = jnp.dot(rows, whole, precision=lax.Precision.HIGHEST)
    return (matched_values, ref_out)


def solution(mesh):
    return jax.shard_map(
        per_device,
        mesh=mesh,
        in_specs=(
            P(("head", "seq"), None),
            P(("head", "seq"), None),
            P(("head", "seq"), None),
            P(("head", "seq")),
            P("head"),
            P("head"),
        ),
        out_specs=(P("head", None), P(("head", "seq"), None)),
        check_vma=False,
    )
```

```python
import functools
import math

import jax
import jax.numpy as jnp
from jax import lax
from jax.experimental import pallas as pl
from jax.experimental.pallas import tpu as pltpu
from jax.sharding import PartitionSpec as P

SEQ = "seq"
FULL = 32767.0
FINE = 65536.0
LOWEST = -28


def swap(blocks):
    return lax.all_to_all(blocks, SEQ, 0, 0, tiled=True)


def code_of(x):
    x = x.astype(jnp.float32)
    size = jnp.abs(x)
    step = jnp.zeros(x.shape, jnp.int32)
    unit = jnp.full(x.shape, 2.0 ** (7 - LOWEST), jnp.float32)
    for e in range(LOWEST + 1, 3):
        reached = size >= 2.0**e
        step = jnp.where(reached, e - LOWEST, step)
        unit = jnp.where(reached, 2.0 ** (7 - e), unit)
    digits = (size * unit).astype(jnp.int32)
    code = jnp.where(size >= 2.0**LOWEST, step * 128 + digits, 0)
    return jnp.where(x < 0, -code, code).astype(jnp.float32)


def decoded(code):
    code = code.astype(jnp.int32)
    size = jnp.maximum(jnp.abs(code) - 128, 0)
    step = size >> 7
    digits = jnp.where(code == 0, 0, (size & 127) + 128)
    value = digits.astype(jnp.float32) * jnp.left_shift(jnp.int32(1), step).astype(jnp.float32)
    value = value * 2.0 ** (LOWEST - 7)
    return jnp.where(code < 0, -value, value).astype(jnp.bfloat16)


def in_two(x):
    high = x.astype(jnp.bfloat16)
    return high, (x - high.astype(jnp.float32)).astype(jnp.bfloat16)


def product(a, b, dims):
    def one(u, v):
        return lax.dot_general(u, v, (dims, ((), ())), preferred_element_type=jnp.float32)

    return one(a[0], b[0]) + (one(a[0], b[1]) + one(a[1], b[0]))


ROWS = ((1,), (0,))
BY_ROW = ((0,), (0,))
BY_COLUMN = ((1,), (1,))


def solve_kernel(level_ref, queries_ref, kept_ref, out_ref, system_ref, weights_ref, inverse_ref, rest_ref):
    size = system_ref.shape[0]
    inv_root = 1.0 / math.sqrt(queries_ref.shape[1])
    logits = lax.dot_general(
        queries_ref[...], kept_ref[...], (BY_COLUMN, ((), ())), preferred_element_type=jnp.float32
    ) * inv_root
    weights = jnp.exp(logits - jnp.max(logits, axis=1, keepdims=True))
    weights = weights / jnp.sum(weights, axis=1, keepdims=True)
    weights_ref[...] = weights
    parts = in_two(weights)
    gram = product(parts, parts, BY_ROW)
    ridge = level_ref[0].astype(jnp.float32) * 0.01
    bound = jnp.max(jnp.sum(weights, axis=0, keepdims=True), axis=1, keepdims=True) * 1.0001
    row = lax.broadcasted_iota(jnp.int32, (size, size), 0)
    column = lax.broadcasted_iota(jnp.int32, (size, size), 1)
    eye = jnp.where(row == column, 1.0, 0.0)
    system = gram + ridge * eye
    system_ref[...] = system
    span = jnp.max(bound) + 2.0 * ridge
    first = 2.0 / span
    rest = eye - first * system
    rest_ref[...] = rest
    inverse_ref[...] = first * eye
    reach = span / jnp.max(bound)

    def step(reach):
        ahead = 2.0 * reach * reach
        scale = ahead / (ahead - 1.0)
        rest = in_two(rest_ref[...])
        inverse = inverse_ref[...]
        inverse_ref[...] = scale * (inverse + product(in_two(inverse), rest, ROWS))
        rest_ref[...] = scale * product(rest, rest, ROWS) - (scale - 1.0) * eye
        return ahead - 1.0

    lax.while_loop(lambda reach: reach < 4096.0, step, reach)
    inverse = inverse_ref[...]
    rest = eye - jnp.dot(
        system_ref[...], inverse, precision=lax.Precision.HIGHEST, preferred_element_type=jnp.float32
    )
    inverse = inverse + product(in_two(inverse), in_two(rest), ROWS)
    out_ref[...] = product(in_two(inverse), in_two(weights_ref[...]), BY_COLUMN)


def solve_rows(level, queries, kept):
    count, size = queries.shape[0], kept.shape[0]
    vmem = pl.BlockSpec(memory_space=pltpu.VMEM)
    return pl.pallas_call(
        solve_kernel,
        out_shape=jax.ShapeDtypeStruct((size, count), jnp.float32),
        in_specs=[pl.BlockSpec(memory_space=pltpu.SMEM), vmem, vmem],
        out_specs=vmem,
        scratch_shapes=[
            pltpu.VMEM((size, size), jnp.float32),
            pltpu.VMEM((count, size), jnp.float32),
            pltpu.VMEM((size, size), jnp.float32),
            pltpu.VMEM((size, size), jnp.float32),
        ],
        compiler_params=pltpu.CompilerParams(vmem_limit_bytes=40 * 2**20),
        cost_estimate=pl.CostEstimate(flops=12 * 10**9, bytes_accessed=2 * 2**20, transcendentals=2**18),
        name="solve",
    )(level, queries, kept)


def pick_kernel(start_ref, positions_ref, kept_ref, keys_ref, queries_ref, out_ref):
    slab_len, head_dim = keys_ref.shape
    peers = out_ref.shape[0]
    own_count = positions_ref.shape[0]
    start = start_ref[0]
    lane = lax.broadcasted_iota(jnp.int32, (1, head_dim), 1)

    def one_hot(places):
        return jnp.concatenate(
            [
                jnp.where(places == (lane + at).astype(jnp.float32), 1.0, 0.0).astype(jnp.bfloat16)
                for at in range(0, slab_len, head_dim)
            ],
            axis=1,
        )

    offset = (kept_ref[...] - start).astype(jnp.float32)
    offset = jnp.transpose(jnp.broadcast_to(offset, (head_dim, offset.shape[1])))
    picked = jnp.dot(one_hot(offset), keys_ref[...], preferred_element_type=jnp.float32)
    row = lax.broadcasted_iota(jnp.int32, (2 * own_count, head_dim), 0)
    place = jnp.full((2 * own_count, head_dim), -1, jnp.int32)
    for k in range(own_count):
        place = jnp.where(row == k, positions_ref[k] - start, place)
    own = jnp.dot(one_hot(place.astype(jnp.float32)), queries_ref[...], preferred_element_type=jnp.float32)
    own = jnp.broadcast_to(own[None, :own_count], (peers, own_count, head_dim))
    picked = picked.reshape(peers, -1, head_dim)
    out_ref[...] = jnp.concatenate([own, picked], axis=1).astype(jnp.bfloat16)


def in_words(x):
    whole = jnp.floor(x)
    fine = jnp.minimum(jnp.round((x - whole) * FINE), FINE - 1.0) - FINE / 2
    return whole, fine


def power_of_two(k):
    return jnp.exp(k * math.log(2.0))


def attend_kernel(own_count, got_ref, keys_ref, values_ref, queries_ref, coarse_ref, marks_ref, code_ref):
    head_dim = keys_ref.shape[1]
    peers = got_ref.shape[0]
    rows = peers * own_count
    inv_root = 1.0 / math.sqrt(head_dim)
    got = got_ref[...].astype(jnp.float32)
    code_ref[...] = code_of(jnp.sum(got[:, own_count:], axis=0))
    queries_ref[...] = got[:, :own_count].reshape(rows, head_dim).astype(jnp.bfloat16)
    block = rows // 2
    for at in range(0, rows, block):
        scores = lax.dot_general(
            queries_ref[at : at + block], keys_ref[...], (BY_COLUMN, ((), ())), preferred_element_type=jnp.float32
        ) * inv_root
        peak = jnp.max(scores, axis=1, keepdims=True)
        probs = jnp.exp(scores - peak).astype(jnp.bfloat16)
        total = jnp.sum(probs.astype(jnp.float32), axis=1, keepdims=True)
        mean = jnp.dot(probs, values_ref[...], preferred_element_type=jnp.float32) / total
        most = jnp.max(jnp.abs(mean), axis=1, keepdims=True)
        power = jnp.ceil(jnp.log(jnp.maximum(most, 2.0**-58)) / math.log(2.0))
        coarse_ref[at : at + block] = jnp.clip(jnp.round(mean / power_of_two(power) * FULL), -FULL, FULL)
        peak_whole, peak_fine = in_words(peak)
        sent_peak = peak_whole + (peak_fine + FINE / 2) / FINE
        share_whole, share_fine = in_words(jnp.log(total) + (peak - sent_peak))
        lane = lax.broadcasted_iota(jnp.int32, (block, head_dim), 1)
        row = lax.broadcasted_iota(jnp.int32, (block, head_dim), 0)
        place = lane - (row & (own_count - 1))
        marks = jnp.zeros((block, head_dim), jnp.float32)
        for k, mark in enumerate((peak_whole, peak_fine, share_whole, share_fine, power)):
            marks = jnp.where(place == k * own_count, mark, marks)
        marks = jnp.sum(marks.reshape(block // own_count, own_count, head_dim), axis=1)
        marks_ref[at // own_count : (at + block) // own_count] = marks


def per_device(keys, values, queries, query_positions, kept_index, ridge_level):
    slab_len, head_dim = keys.shape
    own_count = query_positions.shape[0]
    peers = lax.axis_size(SEQ)
    own_kept = kept_index.shape[0] // peers
    vmem = pl.BlockSpec(memory_space=pltpu.VMEM)
    smem = pl.BlockSpec(memory_space=pltpu.SMEM)
    roomy = pltpu.CompilerParams(vmem_limit_bytes=40 * 2**20)
    slab_start = (lax.axis_index(SEQ) * slab_len).astype(jnp.int32).reshape(1)
    sent = pl.pallas_call(
        pick_kernel,
        out_shape=jax.ShapeDtypeStruct((peers, own_count + own_kept, head_dim), jnp.bfloat16),
        in_specs=[smem, smem, vmem, vmem, vmem],
        out_specs=vmem,
        compiler_params=roomy,
        name="pick",
    )(slab_start, query_positions, kept_index[None], keys, queries)
    got = swap(sent)
    rows = peers * own_count
    all_queries, coarse, marks, code = pl.pallas_call(
        functools.partial(attend_kernel, own_count),
        out_shape=[
            jax.ShapeDtypeStruct((rows, head_dim), jnp.bfloat16),
            jax.ShapeDtypeStruct((rows, head_dim), jnp.float32),
            jax.ShapeDtypeStruct((peers, head_dim), jnp.float32),
            jax.ShapeDtypeStruct((own_kept, head_dim), jnp.float32),
        ],
        in_specs=[vmem] * 3,
        out_specs=[vmem] * 4,
        compiler_params=roomy,
        name="attend",
    )(got, keys, values)
    sent = jnp.concatenate(
        [
            coarse.reshape(peers, own_count // 2, 2, head_dim),
            jnp.broadcast_to(code.reshape(own_kept // 2, 2, head_dim), (peers, own_kept // 2, 2, head_dim)),
            jnp.pad(marks.reshape(peers, 1, 1, head_dim), ((0, 0), (0, 0), (0, 1), (0, 0))),
        ],
        axis=1,
    ).astype(jnp.int16)
    got = swap(sent)
    kept_keys = decoded(got[:, own_count // 2 : (own_count + own_kept) // 2]).reshape(peers * own_kept, head_dim)
    marks = got[:, -1, 0].astype(jnp.float32)
    marks = [marks[:, k * own_count : (k + 1) * own_count] for k in range(5)]
    peaks = marks[0] + (marks[1] + FINE / 2) / FINE
    shares = marks[2] + (marks[3] + FINE / 2) / FINE
    factors = jnp.exp(peaks - jnp.max(peaks, axis=0)[None] + shares)
    scales = factors * power_of_two(marks[4]) / FULL / jnp.sum(factors, axis=0)[None]
    means = got[:, : own_count // 2].reshape(peers, own_count, head_dim).astype(jnp.float32)
    ref_out = jnp.sum(means * scales[:, :, None], axis=0)

    most = jnp.max(jnp.abs(ref_out), axis=1, keepdims=True)
    power = jnp.ceil(jnp.log(jnp.maximum(most, 2.0**-58)) / math.log(2.0))
    coarse = jnp.clip(jnp.round(ref_out / power_of_two(power) * FULL), -FULL, FULL)
    power = jnp.pad(power.reshape(1, own_count), ((0, 1), (0, head_dim - own_count)))
    sent = jnp.concatenate([coarse, power], axis=0).reshape(1, own_count // 2 + 1, 2, head_dim).astype(jnp.int16)
    whole = swap(jnp.broadcast_to(sent, (peers, *sent.shape[1:])))
    answer = solve_rows(ridge_level, all_queries, kept_keys)
    power = whole[:, -1, 0, :own_count].astype(jnp.float32)
    whole = whole[:, :-1].reshape(peers, own_count, head_dim).astype(jnp.float32)
    whole = (whole * (power_of_two(power) / FULL)[:, :, None]).reshape(rows, head_dim)
    matched_values = jnp.dot(answer, whole, precision=lax.Precision.HIGH)
    return (matched_values, ref_out)


def solution(mesh):
    return jax.shard_map(
        per_device,
        mesh=mesh,
        in_specs=(
            P(("head", "seq"), None),
            P(("head", "seq"), None),
            P(("head", "seq"), None),
            P(("head", "seq")),
            P("head"),
            P("head"),
        ),
        out_specs=(P("head", None), P(("head", "seq"), None)),
        check_vma=False,
    )
```

```python
import functools
import math

import jax
import jax.numpy as jnp
from jax import lax
from jax.experimental import pallas as pl
from jax.experimental.pallas import tpu as pltpu
from jax.sharding import PartitionSpec as P

SEQ = "seq"
FULL = 32767.0
PEAK_UNIT = 2.0**17
SHARE_UNIT = 2.0**26
LANES = 128
TILE = 16
KEY_PARTS = 4
LOWEST = -28


def swap(blocks):
    return lax.all_to_all(blocks, SEQ, 0, 0, tiled=True)


def code_of(x):
    x = x.astype(jnp.float32)
    size = jnp.abs(x)
    step = jnp.zeros(x.shape, jnp.int32)
    unit = jnp.full(x.shape, 2.0 ** (7 - LOWEST), jnp.float32)
    for e in range(LOWEST + 1, 3):
        reached = size >= 2.0**e
        step = jnp.where(reached, e - LOWEST, step)
        unit = jnp.where(reached, 2.0 ** (7 - e), unit)
    digits = (size * unit).astype(jnp.int32)
    code = jnp.where(size >= 2.0**LOWEST, step * 128 + digits, 0)
    return jnp.where(x < 0, -code, code)


def decoded(code):
    size = jnp.maximum(jnp.abs(code) - 128, 0)
    step = size >> 7
    digits = jnp.where(code == 0, 0, (size & 127) + 128)
    value = digits.astype(jnp.float32) * jnp.left_shift(jnp.int32(1), step).astype(jnp.float32)
    value = value * 2.0 ** (LOWEST - 7)
    return jnp.where(code < 0, -value, value)


def packed(high, low):
    return (high << 16) | (low & 0xFFFF)


def high_of(word):
    return word >> 16


def low_of(word):
    return (word << 16) >> 16


def every(ref, first, stride):
    return ref[pl.ds(first, ref.shape[0] // stride, stride=stride)]


def power_of_two(k):
    return jnp.exp(k * math.log(2.0))


def scaled(x):
    most = jnp.max(jnp.abs(x), axis=1, keepdims=True)
    power = jnp.ceil(jnp.log(jnp.maximum(most, 2.0**-58)) / math.log(2.0))
    whole = jnp.clip(jnp.round(x / power_of_two(power) * FULL), -FULL, FULL)
    return whole.astype(jnp.int32), power


def in_lanes(columns, own_count):
    rows = columns[0].shape[0]
    lane = lax.broadcasted_iota(jnp.int32, (rows, LANES), 1)
    row = lax.broadcasted_iota(jnp.int32, (rows, LANES), 0)
    place = lane - (row & (own_count - 1))
    marks = jnp.zeros((rows, LANES), jnp.float32)
    for k, column in enumerate(columns):
        marks = jnp.where(place == k * own_count, column, marks)
    return jnp.sum(marks.reshape(rows // own_count, own_count, LANES), axis=1)


def in_two(x):
    high = x.astype(jnp.bfloat16)
    return high, (x - high.astype(jnp.float32)).astype(jnp.bfloat16)


def product(a, b, dims):
    def one(u, v):
        return lax.dot_general(u, v, (dims, ((), ())), preferred_element_type=jnp.float32)

    return one(a[0], b[0]) + (one(a[0], b[1]) + one(a[1], b[0]))


ROWS = ((1,), (0,))
BY_ROW = ((0,), (0,))
BY_COLUMN = ((1,), (1,))


def solve_kernel(own_count, level_ref, queries_ref, words_ref, high_ref, low_ref, kept_ref, system_ref, weights_ref, inverse_ref, rest_ref):
    size = system_ref.shape[0]
    inv_root = 1.0 / math.sqrt(queries_ref.shape[1])
    for k in range(own_count):
        kept_ref[pl.ds(k, size // own_count, stride=own_count)] = decoded(low_of(every(words_ref, k, own_count + 1)))
    kept = kept_ref[...].astype(jnp.bfloat16)
    logits = lax.dot_general(
        queries_ref[...], kept, (BY_COLUMN, ((), ())), preferred_element_type=jnp.float32
    ) * inv_root
    weights = jnp.exp(logits - jnp.max(logits, axis=1, keepdims=True))
    weights = weights / jnp.sum(weights, axis=1, keepdims=True)
    weights_ref[...] = weights
    parts = in_two(weights)
    gram = product(parts, parts, BY_ROW)
    ridge = level_ref[0].astype(jnp.float32) * 0.01
    bound = jnp.max(jnp.sum(weights, axis=0, keepdims=True), axis=1, keepdims=True) * 1.0001
    row = lax.broadcasted_iota(jnp.int32, (size, size), 0)
    column = lax.broadcasted_iota(jnp.int32, (size, size), 1)
    eye = jnp.where(row == column, 1.0, 0.0)
    system = gram + ridge * eye
    system_ref[...] = system
    span = jnp.max(bound) + 2.0 * ridge
    first = 2.0 / span
    rest = eye - first * system
    rest_ref[...] = rest
    inverse_ref[...] = first * eye
    reach = span / jnp.max(bound)

    def step(reach):
        ahead = 2.0 * reach * reach
        scale = ahead / (ahead - 1.0)
        rest = in_two(rest_ref[...])
        inverse = inverse_ref[...]
        inverse_ref[...] = scale * (inverse + product(in_two(inverse), rest, ROWS))
        rest_ref[...] = scale * product(rest, rest, ROWS) - (scale - 1.0) * eye
        return ahead - 1.0

    lax.while_loop(lambda reach: reach < 4096.0, step, reach)
    inverse = inverse_ref[...]
    rest = eye - jnp.dot(
        system_ref[...], inverse, precision=lax.Precision.HIGHEST, preferred_element_type=jnp.float32
    )
    inverse = inverse + product(in_two(inverse), in_two(rest), ROWS)
    high_ref[...], low_ref[...] = in_two(product(in_two(inverse), in_two(weights_ref[...]), BY_COLUMN))


def pick_kernel(start_ref, positions_ref, kept_hbm, keys_hbm, queries_hbm, out_ref, kept_ref, keys_ref, near_ref, sems, near_sems):
    slab_len = keys_ref.shape[0]
    peers = out_ref.shape[0]
    own_count = positions_ref.shape[0]
    start = start_ref[0]
    tile = near_ref.shape[0] // own_count
    rest = keys_ref.shape[0] // KEY_PARTS
    copies = [pltpu.make_async_copy(kept_hbm, kept_ref, sems.at[KEY_PARTS])]
    for k in range(KEY_PARTS):
        part = pl.ds(k * rest, rest)
        copies.append(pltpu.make_async_copy(keys_hbm.at[part], keys_ref.at[part], sems.at[k]))
    places = [jnp.clip(positions_ref[k] - start, 0, slab_len - 1) for k in range(own_count)]
    near = []
    for k in range(own_count):
        first = pl.multiple_of((places[k] // tile) * tile, tile)
        near.append(pltpu.make_async_copy(queries_hbm.at[pl.ds(first, tile)], near_ref.at[pl.ds(k * tile, tile)], near_sems.at[k]))
    for copy in copies + near:
        copy.start()
    lane = lax.broadcasted_iota(jnp.int32, (1, LANES), 1)

    def one_hot(places, size):
        return jnp.concatenate(
            [
                jnp.where(places == (lane + at).astype(jnp.float32), 1.0, 0.0).astype(jnp.bfloat16)
                for at in range(0, size, LANES)
            ],
            axis=1,
        )

    row = lax.broadcasted_iota(jnp.int32, (2 * own_count, LANES), 0)
    place = jnp.full((2 * own_count, LANES), -1, jnp.int32)
    for k in range(own_count):
        place = jnp.where(row == k, k * tile + places[k] % tile, place)
    copies[0].wait()
    offset = (kept_ref[...] - start).astype(jnp.float32)
    offset = jnp.transpose(jnp.broadcast_to(offset, (LANES, offset.shape[1])))
    chosen = one_hot(offset, slab_len)
    for copy in near:
        copy.wait()
    own = jnp.dot(one_hot(place.astype(jnp.float32), own_count * tile), near_ref[...], preferred_element_type=jnp.float32)
    own = jnp.broadcast_to(own[None, :own_count], (peers, own_count, LANES))
    for copy in copies[1:]:
        copy.wait()
    picked = jnp.dot(chosen, keys_ref[...], preferred_element_type=jnp.float32)
    picked = picked.reshape(peers, -1, LANES)
    out_ref[...] = jnp.concatenate([own, picked], axis=1).astype(jnp.bfloat16)


def attend_kernel(own_count, got_ref, keys_ref, values_ref, queries_ref, out_ref, word_ref, mark_ref):
    peers = got_ref.shape[0]
    rows = peers * own_count
    inv_root = 1.0 / math.sqrt(keys_ref.shape[1])
    got = got_ref[...].astype(jnp.float32)
    code = code_of(jnp.sum(got[:, own_count:], axis=0))
    queries_ref[...] = got[:, :own_count].reshape(rows, LANES).astype(jnp.bfloat16)
    block = rows // 2
    for at in range(0, rows, block):
        scores = lax.dot_general(
            queries_ref[at : at + block], keys_ref[...], (BY_COLUMN, ((), ())), preferred_element_type=jnp.float32
        ) * inv_root
        peak = jnp.max(scores, axis=1, keepdims=True)
        probs = jnp.exp(scores - peak).astype(jnp.bfloat16)
        total = jnp.sum(probs.astype(jnp.float32), axis=1, keepdims=True)
        mean = jnp.dot(probs, values_ref[...], preferred_element_type=jnp.float32) / total
        whole, power = scaled(mean)
        words = packed(whole.reshape(block // own_count, own_count, LANES), code[None])
        word_ref[at : at + block] = words.reshape(block, LANES)
        peak_mark = jnp.round(peak * PEAK_UNIT)
        share_mark = jnp.round((jnp.log(total) + (peak - peak_mark / PEAK_UNIT)) * SHARE_UNIT)
        marks = in_lanes((peak_mark, share_mark, power), own_count)
        mark_ref[at // own_count : (at + block) // own_count] = marks.astype(jnp.int32)
    for k in range(own_count):
        out_ref[pl.ds(k, peers, stride=own_count + 1)] = every(word_ref, k, own_count)
    out_ref[pl.ds(own_count, peers, stride=own_count + 1)] = mark_ref[...]


def merge_kernel(words_ref, ref_out_ref, out_ref):
    own_count = ref_out_ref.shape[0]
    marks = every(words_ref, own_count, own_count + 1).astype(jnp.float32)
    peaks = marks[:, :own_count] / PEAK_UNIT
    shares = marks[:, own_count : 2 * own_count] / SHARE_UNIT
    powers = marks[:, 2 * own_count : 3 * own_count]
    factors = jnp.exp(peaks - jnp.max(peaks, axis=0, keepdims=True) + shares)
    scales = factors * power_of_two(powers) * (1.0 / FULL) / jnp.sum(factors, axis=0, keepdims=True)
    ref_out = jnp.concatenate(
        [
            jnp.sum(
                high_of(every(words_ref, k, own_count + 1)).astype(jnp.float32) * scales[:, k : k + 1],
                axis=0,
                keepdims=True,
            )
            for k in range(own_count)
        ],
        axis=0,
    )
    ref_out_ref[...] = ref_out
    whole, power = scaled(ref_out)
    half = own_count // 2
    words = packed(whole[:half], whole[half:])
    words = jnp.concatenate([words, in_lanes((power,), own_count).astype(jnp.int32)], axis=0)
    peers = out_ref.shape[0] // (half + 1)
    for k in range(half + 1):
        out_ref[pl.ds(k, peers, stride=half + 1)] = jnp.broadcast_to(words[k : k + 1], (peers, LANES))


def finish_kernel(own_count, words_ref, high_ref, low_ref, out_ref, rows_ref):
    half = own_count // 2
    peers = words_ref.shape[0] // (half + 1)
    scales = power_of_two(every(words_ref, half, half + 1).astype(jnp.float32)[:, :own_count]) * (1.0 / FULL)
    for k in range(own_count):
        words = every(words_ref, k % half, half + 1)
        whole = high_of(words) if k < half else low_of(words)
        rows_ref[pl.ds(k, peers, stride=own_count)] = whole.astype(jnp.float32) * scales[:, k : k + 1]
    out_ref[...] = product((high_ref[...], low_ref[...]), in_two(rows_ref[...]), ROWS)


def per_device(keys, values, queries, query_positions, kept_index, ridge_level):
    slab_len, head_dim = keys.shape
    own_count = query_positions.shape[0]
    kept_count = kept_index.shape[0]
    peers = lax.axis_size(SEQ)
    own_kept = kept_count // peers
    rows = peers * own_count
    vmem = pl.BlockSpec(memory_space=pltpu.VMEM)
    smem = pl.BlockSpec(memory_space=pltpu.SMEM)
    hbm = pl.BlockSpec(memory_space=pltpu.HBM)
    roomy = pltpu.CompilerParams(vmem_limit_bytes=24 * 2**20)
    whole = pltpu.CompilerParams(vmem_limit_bytes=60 * 2**20)
    small = pltpu.CompilerParams(vmem_limit_bytes=8 * 2**20)
    f32, bf16, i32 = jnp.float32, jnp.bfloat16, jnp.int32
    slab_start = (lax.axis_index(SEQ) * slab_len).astype(i32).reshape(1)
    sent = pl.pallas_call(
        pick_kernel,
        out_shape=jax.ShapeDtypeStruct((peers, own_count + own_kept, head_dim), bf16),
        in_specs=[smem, smem, hbm, hbm, hbm],
        out_specs=vmem,
        scratch_shapes=[
            pltpu.VMEM((1, kept_count), i32),
            pltpu.VMEM((slab_len, head_dim), bf16),
            pltpu.VMEM((own_count * TILE, head_dim), bf16),
            pltpu.SemaphoreType.DMA((KEY_PARTS + 1,)),
            pltpu.SemaphoreType.DMA((own_count,)),
        ],
        compiler_params=whole,
        name="pick",
    )(slab_start, query_positions, kept_index[None], keys, queries)
    got = swap(sent)
    all_queries, words = pl.pallas_call(
        functools.partial(attend_kernel, own_count),
        out_shape=[
            jax.ShapeDtypeStruct((rows, head_dim), bf16),
            jax.ShapeDtypeStruct((peers * (own_count + 1), LANES), i32),
        ],
        in_specs=[vmem] * 3,
        out_specs=[vmem] * 2,
        scratch_shapes=[pltpu.VMEM((rows, head_dim), i32), pltpu.VMEM((peers, LANES), i32)],
        compiler_params=roomy,
        name="attend",
    )(got, keys, values)
    words = swap(words.reshape(peers, own_count + 1, 1, LANES)).reshape(words.shape)
    ref_out, means = pl.pallas_call(
        merge_kernel,
        out_shape=[
            jax.ShapeDtypeStruct((own_count, head_dim), f32),
            jax.ShapeDtypeStruct((peers * (own_count // 2 + 1), LANES), i32),
        ],
        in_specs=[vmem],
        out_specs=[vmem] * 2,
        compiler_params=small,
        name="merge",
    )(words)
    means = swap(means.reshape(peers, own_count // 2 + 1, 1, LANES)).reshape(means.shape)
    square = (kept_count, kept_count)
    high, low = pl.pallas_call(
        functools.partial(solve_kernel, own_count),
        out_shape=[jax.ShapeDtypeStruct((kept_count, rows), bf16)] * 2,
        in_specs=[smem, vmem, vmem],
        out_specs=[vmem] * 2,
        scratch_shapes=[
            pltpu.VMEM((kept_count, head_dim), f32),
            pltpu.VMEM(square, f32),
            pltpu.VMEM((rows, kept_count), f32),
            pltpu.VMEM(square, f32),
            pltpu.VMEM(square, f32),
        ],
        compiler_params=roomy,
        cost_estimate=pl.CostEstimate(flops=12 * 10**9, bytes_accessed=2 * 2**20, transcendentals=2**18),
        name="solve",
    )(ridge_level, all_queries, words)
    matched_values = pl.pallas_call(
        functools.partial(finish_kernel, own_count),
        out_shape=jax.ShapeDtypeStruct((kept_count, head_dim), f32),
        in_specs=[vmem] * 3,
        out_specs=vmem,
        scratch_shapes=[pltpu.VMEM((rows, head_dim), f32)],
        compiler_params=roomy,
        name="finish",
    )(means, high, low)
    return (matched_values, ref_out)


def solution(mesh):
    return jax.shard_map(
        per_device,
        mesh=mesh,
        in_specs=(
            P(("head", "seq"), None),
            P(("head", "seq"), None),
            P(("head", "seq"), None),
            P(("head", "seq")),
            P("head"),
            P("head"),
        ),
        out_specs=(P("head", None), P(("head", "seq"), None)),
        check_vma=False,
    )
```

```python
import functools
import math

import jax
import jax.numpy as jnp
from jax import lax
from jax.experimental import pallas as pl
from jax.experimental.pallas import tpu as pltpu
from jax.sharding import PartitionSpec as P

SEQ = "seq"
FULL = 32767.0
PEAK_UNIT = 2.0**17
SHARE_UNIT = 2.0**26
LANES = 128
TILE = 16
KEY_PARTS = 4
LOWEST = -28


def swap(blocks):
    return lax.all_to_all(blocks, SEQ, 0, 0, tiled=True)


def code_of(x):
    x = x.astype(jnp.float32)
    size = jnp.abs(x)
    step = jnp.zeros(x.shape, jnp.int32)
    unit = jnp.full(x.shape, 2.0 ** (7 - LOWEST), jnp.float32)
    for e in range(LOWEST + 1, 3):
        reached = size >= 2.0**e
        step = jnp.where(reached, e - LOWEST, step)
        unit = jnp.where(reached, 2.0 ** (7 - e), unit)
    digits = (size * unit).astype(jnp.int32)
    code = jnp.where(size >= 2.0**LOWEST, step * 128 + digits, 0)
    return jnp.where(x < 0, -code, code)


def decoded(code):
    size = jnp.maximum(jnp.abs(code) - 128, 0)
    step = size >> 7
    digits = jnp.where(code == 0, 0, (size & 127) + 128)
    value = digits.astype(jnp.float32) * jnp.left_shift(jnp.int32(1), step).astype(jnp.float32)
    value = value * 2.0 ** (LOWEST - 7)
    return jnp.where(code < 0, -value, value)


def packed(high, low):
    return (high << 16) | (low & 0xFFFF)


def high_of(word):
    return word >> 16


def low_of(word):
    return (word << 16) >> 16


def every(ref, first, stride):
    return ref[pl.ds(first, ref.shape[0] // stride, stride=stride)]


def power_of_two(k):
    return jnp.exp(k * math.log(2.0))


def scaled(x):
    most = jnp.max(jnp.abs(x), axis=1, keepdims=True)
    power = jnp.ceil(jnp.log(jnp.maximum(most, 2.0**-58)) / math.log(2.0))
    whole = jnp.clip(jnp.round(x / power_of_two(power) * FULL), -FULL, FULL)
    return whole.astype(jnp.int32), power


def in_lanes(columns, own_count):
    rows = columns[0].shape[0]
    lane = lax.broadcasted_iota(jnp.int32, (rows, LANES), 1)
    row = lax.broadcasted_iota(jnp.int32, (rows, LANES), 0)
    place = lane - (row & (own_count - 1))
    marks = jnp.zeros((rows, LANES), jnp.float32)
    for k, column in enumerate(columns):
        marks = jnp.where(place == k * own_count, column, marks)
    return jnp.sum(marks.reshape(rows // own_count, own_count, LANES), axis=1)


def in_two(x):
    high = x.astype(jnp.bfloat16)
    return high, (x - high.astype(jnp.float32)).astype(jnp.bfloat16)


def product(a, b, dims):
    def one(u, v):
        return lax.dot_general(u, v, (dims, ((), ())), preferred_element_type=jnp.float32)

    return one(a[0], b[0]) + (one(a[0], b[1]) + one(a[1], b[0]))


ROWS = ((1,), (0,))
BY_ROW = ((0,), (0,))
BY_COLUMN = ((1,), (1,))


def solve_kernel(own_count, level_ref, queries_ref, words_ref, high_ref, low_ref, kept_ref, system_ref, weights_ref, inverse_ref, rest_ref):
    size = system_ref.shape[0]
    inv_root = 1.0 / math.sqrt(queries_ref.shape[1])
    for k in range(own_count):
        kept_ref[pl.ds(k, size // own_count, stride=own_count)] = decoded(low_of(every(words_ref, k, own_count + 1)))
    kept = kept_ref[...].astype(jnp.bfloat16)
    logits = lax.dot_general(
        queries_ref[...], kept, (BY_COLUMN, ((), ())), preferred_element_type=jnp.float32
    ) * inv_root
    weights = jnp.exp(logits - jnp.max(logits, axis=1, keepdims=True))
    weights = weights / jnp.sum(weights, axis=1, keepdims=True)
    weights_ref[...] = weights
    parts = in_two(weights)
    gram = product(parts, parts, BY_ROW)
    ridge = level_ref[0].astype(jnp.float32) * 0.01
    bound = jnp.max(jnp.sum(weights, axis=0, keepdims=True), axis=1, keepdims=True) * 1.0001
    row = lax.broadcasted_iota(jnp.int32, (size, size), 0)
    column = lax.broadcasted_iota(jnp.int32, (size, size), 1)
    eye = jnp.where(row == column, 1.0, 0.0)
    system = gram + ridge * eye
    system_ref[...] = system
    span = jnp.max(bound) + 2.0 * ridge
    first = 2.0 / span
    rest = eye - first * system
    rest_ref[...] = rest
    inverse_ref[...] = first * eye
    reach = span / jnp.max(bound)

    def step(reach):
        ahead = 2.0 * reach * reach
        scale = ahead / (ahead - 1.0)
        rest = in_two(rest_ref[...])
        inverse = inverse_ref[...]
        inverse_ref[...] = scale * (inverse + product(in_two(inverse), rest, ROWS))
        rest_ref[...] = scale * product(rest, rest, ROWS) - (scale - 1.0) * eye
        return ahead - 1.0

    lax.while_loop(lambda reach: reach < 4096.0, step, reach)
    inverse = inverse_ref[...]
    rest = eye - jnp.dot(
        system_ref[...], inverse, precision=lax.Precision.HIGHEST, preferred_element_type=jnp.float32
    )
    inverse = inverse + product(in_two(inverse), in_two(rest), ROWS)
    high_ref[...], low_ref[...] = in_two(product(in_two(inverse), in_two(weights_ref[...]), BY_COLUMN))


def sent_out(source, target, sems, first, rows, parts=2):
    size = rows // parts
    copies = []
    for k in range(parts):
        part = pl.ds(first + k * size, size)
        copies.append(pltpu.make_async_copy(source.at[part], target.at[part], sems.at[k]))
        copies[-1].start()
    return copies


def pick_kernel(
    positions_hbm, kept_hbm, keys_hbm, queries_hbm, out_hbm,
    positions_ref, kept_ref, keys_ref, near_ref, out_ref, first_sems, sems, near_sems, out_sems,
):
    slab_len = keys_ref.shape[0]
    peers = out_ref.shape[0]
    own_count = positions_ref.shape[0]
    start = lax.axis_index(SEQ).astype(jnp.int32) * slab_len
    tile = near_ref.shape[0] // own_count
    rest = keys_ref.shape[0] // KEY_PARTS
    positions_copy = pltpu.make_async_copy(positions_hbm, positions_ref, first_sems.at[0])
    kept_copy = pltpu.make_async_copy(kept_hbm, kept_ref, first_sems.at[1])
    positions_copy.start()
    kept_copy.start()
    copies = []
    for k in range(KEY_PARTS):
        part = pl.ds(k * rest, rest)
        copies.append(pltpu.make_async_copy(keys_hbm.at[part], keys_ref.at[part], sems.at[k]))
        copies[-1].start()
    positions_copy.wait()
    places = [jnp.clip(positions_ref[k] - start, 0, slab_len - 1) for k in range(own_count)]
    near = []
    for k in range(own_count):
        first = pl.multiple_of((places[k] // tile) * tile, tile)
        near.append(pltpu.make_async_copy(queries_hbm.at[pl.ds(first, tile)], near_ref.at[pl.ds(k * tile, tile)], near_sems.at[k]))
        near[-1].start()
    lane = lax.broadcasted_iota(jnp.int32, (1, LANES), 1)

    def one_hot(places, size):
        return jnp.concatenate(
            [
                jnp.where(places == (lane + at).astype(jnp.float32), 1.0, 0.0).astype(jnp.bfloat16)
                for at in range(0, size, LANES)
            ],
            axis=1,
        )

    row = lax.broadcasted_iota(jnp.int32, (2 * own_count, LANES), 0)
    place = jnp.full((2 * own_count, LANES), -1, jnp.int32)
    for k in range(own_count):
        place = jnp.where(row == k, k * tile + places[k] % tile, place)
    kept_copy.wait()
    offset = (kept_ref[...] - start).astype(jnp.float32)
    offset = jnp.transpose(jnp.broadcast_to(offset, (LANES, offset.shape[1])))
    chosen = one_hot(offset, slab_len)
    for copy in copies:
        copy.wait()
    picked = jnp.dot(chosen, keys_ref[...], preferred_element_type=jnp.float32)
    picked = picked.reshape(peers, -1, LANES)
    for copy in near:
        copy.wait()
    own = jnp.dot(one_hot(place.astype(jnp.float32), own_count * tile), near_ref[...], preferred_element_type=jnp.float32)
    half = peers // 2
    own = jnp.broadcast_to(own[None, :own_count], (half, own_count, LANES))
    moved = []
    for k in range(2):
        out_ref[k * half : (k + 1) * half] = jnp.concatenate([own, picked[k * half : (k + 1) * half]], axis=1).astype(jnp.bfloat16)
        moved += sent_out(out_ref, out_hbm, out_sems.at[k], k * half, half)
    for copy in moved:
        copy.wait()


def attend_kernel(own_count, got_ref, keys_ref, values_ref, queries_ref, out_ref):
    peers = got_ref.shape[0]
    rows = peers * own_count
    inv_root = 1.0 / math.sqrt(keys_ref.shape[1])
    got = got_ref[...].astype(jnp.float32)
    code = code_of(jnp.sum(got[:, own_count:], axis=0))
    queries_ref[...] = got[:, :own_count].reshape(rows, LANES).astype(jnp.bfloat16)
    block = rows // 2
    stride = own_count + 1
    for at in range(0, rows, block):
        scores = lax.dot_general(
            queries_ref[at : at + block], keys_ref[...], (BY_COLUMN, ((), ())), preferred_element_type=jnp.float32
        )
        peak = jnp.max(scores, axis=1, keepdims=True)
        probs = jnp.exp2((scores - peak) * (inv_root * math.log2(math.e))).astype(jnp.bfloat16)
        peak = peak * inv_root
        total = jnp.sum(probs.astype(jnp.float32), axis=1, keepdims=True)
        whole, power = scaled(jnp.dot(probs, values_ref[...], preferred_element_type=jnp.float32) / total)
        peak_mark = jnp.round(peak * PEAK_UNIT)
        share_mark = jnp.round((jnp.log(total) + (peak - peak_mark / PEAK_UNIT)) * SHARE_UNIT)
        marks = in_lanes((peak_mark, share_mark, power), own_count)
        count = block // own_count
        first = at // own_count * stride
        for k in range(count):
            words = packed(whole[k * own_count : (k + 1) * own_count], code)
            out_ref[first + k * stride : first + k * stride + own_count] = words
        out_ref[pl.ds(first + own_count, count, stride=stride)] = marks.astype(jnp.int32)


def merge_kernel(words_ref, ref_out_ref, out_ref):
    own_count = ref_out_ref.shape[0]
    marks = every(words_ref, own_count, own_count + 1).astype(jnp.float32)
    peaks = marks[:, :own_count] / PEAK_UNIT
    shares = marks[:, own_count : 2 * own_count] / SHARE_UNIT
    powers = marks[:, 2 * own_count : 3 * own_count]
    factors = jnp.exp(peaks - jnp.max(peaks, axis=0, keepdims=True) + shares)
    scales = factors * power_of_two(powers) * (1.0 / FULL) / jnp.sum(factors, axis=0, keepdims=True)
    ref_out = jnp.concatenate(
        [
            jnp.sum(
                high_of(every(words_ref, k, own_count + 1)).astype(jnp.float32) * scales[:, k : k + 1],
                axis=0,
                keepdims=True,
            )
            for k in range(own_count)
        ],
        axis=0,
    )
    ref_out_ref[...] = ref_out
    whole, power = scaled(ref_out)
    half = own_count // 2
    words = packed(whole[:half], whole[half:])
    words = jnp.concatenate([words, in_lanes((power,), own_count).astype(jnp.int32)], axis=0)
    peers = out_ref.shape[0] // (half + 1)
    for k in range(peers):
        out_ref[k * (half + 1) : (k + 1) * (half + 1)] = words


def finish_kernel(own_count, words_ref, high_ref, low_ref, out_hbm, out_ref, rows_ref, sems):
    half = own_count // 2
    peers = words_ref.shape[0] // (half + 1)
    scales = power_of_two(every(words_ref, half, half + 1).astype(jnp.float32)[:, :own_count]) * (1.0 / FULL)
    for k in range(own_count):
        words = every(words_ref, k % half, half + 1)
        whole = high_of(words) if k < half else low_of(words)
        rows_ref[pl.ds(k, peers, stride=own_count)] = whole.astype(jnp.float32) * scales[:, k : k + 1]
    high, low = in_two(rows_ref[...])
    both = jnp.concatenate([high, low], axis=1)
    size = out_ref.shape[0] // 2
    moved = []
    for part in range(2):
        at = part * size
        sums = jnp.dot(high_ref[at : at + size], both, preferred_element_type=jnp.float32)
        rest = jnp.dot(low_ref[at : at + size], high, preferred_element_type=jnp.float32)
        out_ref[at : at + size] = sums[:, :LANES] + (sums[:, LANES:] + rest)
        moved += sent_out(out_ref, out_hbm, sems.at[part], at, size)
    for copy in moved:
        copy.wait()


def per_device(keys, values, queries, query_positions, kept_index, ridge_level):
    slab_len, head_dim = keys.shape
    own_count = query_positions.shape[0]
    kept_count = kept_index.shape[0]
    peers = lax.axis_size(SEQ)
    own_kept = kept_count // peers
    rows = peers * own_count
    vmem = pl.BlockSpec(memory_space=pltpu.VMEM)
    smem = pl.BlockSpec(memory_space=pltpu.SMEM)
    hbm = pl.BlockSpec(memory_space=pltpu.HBM)
    roomy = pltpu.CompilerParams(vmem_limit_bytes=24 * 2**20)
    whole = pltpu.CompilerParams(vmem_limit_bytes=60 * 2**20)
    small = pltpu.CompilerParams(vmem_limit_bytes=8 * 2**20)
    f32, bf16, i32 = jnp.float32, jnp.bfloat16, jnp.int32
    sent = pl.pallas_call(
        pick_kernel,
        out_shape=jax.ShapeDtypeStruct((peers, own_count + own_kept, head_dim), bf16),
        in_specs=[hbm] * 4,
        out_specs=hbm,
        scratch_shapes=[
            pltpu.SMEM((own_count,), i32),
            pltpu.VMEM((1, kept_count), i32),
            pltpu.VMEM((slab_len, head_dim), bf16),
            pltpu.VMEM((own_count * TILE, head_dim), bf16),
            pltpu.VMEM((peers, own_count + own_kept, head_dim), bf16),
            pltpu.SemaphoreType.DMA((2,)),
            pltpu.SemaphoreType.DMA((KEY_PARTS,)),
            pltpu.SemaphoreType.DMA((own_count,)),
            pltpu.SemaphoreType.DMA((2, 2)),
        ],
        compiler_params=whole,
        name="pick",
    )(query_positions, kept_index[None], keys, queries)
    got = swap(sent)
    all_queries, words = pl.pallas_call(
        functools.partial(attend_kernel, own_count),
        out_shape=[
            jax.ShapeDtypeStruct((rows, head_dim), bf16),
            jax.ShapeDtypeStruct((peers * (own_count + 1), LANES), i32),
        ],
        in_specs=[vmem] * 3,
        out_specs=[vmem] * 2,
        compiler_params=roomy,
        name="attend",
    )(got, keys, values)
    words = swap(words.reshape(peers, own_count + 1, 1, LANES)).reshape(words.shape)
    ref_out, means = pl.pallas_call(
        merge_kernel,
        out_shape=[
            jax.ShapeDtypeStruct((own_count, head_dim), f32),
            jax.ShapeDtypeStruct((peers * (own_count // 2 + 1), LANES), i32),
        ],
        in_specs=[vmem],
        out_specs=[vmem] * 2,
        compiler_params=small,
        name="merge",
    )(words)
    means = swap(means.reshape(peers, own_count // 2 + 1, 1, LANES)).reshape(means.shape)
    square = (kept_count, kept_count)
    high, low = pl.pallas_call(
        functools.partial(solve_kernel, own_count),
        out_shape=[jax.ShapeDtypeStruct((kept_count, rows), bf16)] * 2,
        in_specs=[smem, vmem, vmem],
        out_specs=[vmem] * 2,
        scratch_shapes=[
            pltpu.VMEM((kept_count, head_dim), f32),
            pltpu.VMEM(square, f32),
            pltpu.VMEM((rows, kept_count), f32),
            pltpu.VMEM(square, f32),
            pltpu.VMEM(square, f32),
        ],
        compiler_params=roomy,
        cost_estimate=pl.CostEstimate(flops=12 * 10**9, bytes_accessed=2 * 2**20, transcendentals=2**18),
        name="solve",
    )(ridge_level, all_queries, words)
    matched_values = pl.pallas_call(
        functools.partial(finish_kernel, own_count),
        out_shape=jax.ShapeDtypeStruct((kept_count, head_dim), f32),
        in_specs=[vmem] * 3,
        out_specs=hbm,
        scratch_shapes=[
            pltpu.VMEM((kept_count, head_dim), f32),
            pltpu.VMEM((rows, head_dim), f32),
            pltpu.SemaphoreType.DMA((2, 2)),
        ],
        compiler_params=roomy,
        name="finish",
    )(means, high, low)
    return (matched_values, ref_out)


def solution(mesh):
    return jax.shard_map(
        per_device,
        mesh=mesh,
        in_specs=(
            P(("head", "seq"), None),
            P(("head", "seq"), None),
            P(("head", "seq"), None),
            P(("head", "seq")),
            P("head"),
            P("head"),
        ),
        out_specs=(P("head", None), P(("head", "seq"), None)),
        check_vma=False,
    )
```

```python
import functools
import math

import jax
import jax.numpy as jnp
from jax import lax
from jax.experimental import pallas as pl
from jax.experimental.pallas import tpu as pltpu
from jax.sharding import PartitionSpec as P

SEQ = "seq"
FULL = 32767.0
PEAK_UNIT = 2.0**17
SHARE_UNIT = 2.0**26
LANES = 128
TILE = 16
KEY_PARTS = 4
LOWEST = -28


def swap(blocks):
    return lax.all_to_all(blocks, SEQ, 0, 0, tiled=True)


def code_of(x):
    x = x.astype(jnp.float32)
    size = jnp.abs(x)
    step = jnp.zeros(x.shape, jnp.int32)
    unit = jnp.full(x.shape, 2.0 ** (7 - LOWEST), jnp.float32)
    for e in range(LOWEST + 1, 3):
        reached = size >= 2.0**e
        step = jnp.where(reached, e - LOWEST, step)
        unit = jnp.where(reached, 2.0 ** (7 - e), unit)
    digits = (size * unit).astype(jnp.int32)
    code = jnp.where(size >= 2.0**LOWEST, step * 128 + digits, 0)
    return jnp.where(x < 0, -code, code)


def decoded(code):
    size = jnp.maximum(jnp.abs(code) - 128, 0)
    step = size >> 7
    digits = jnp.where(code == 0, 0, (size & 127) + 128)
    value = digits.astype(jnp.float32) * jnp.left_shift(jnp.int32(1), step).astype(jnp.float32)
    value = value * 2.0 ** (LOWEST - 7)
    return jnp.where(code < 0, -value, value)


def packed(high, low):
    return (high << 16) | (low & 0xFFFF)


def high_of(word):
    return word >> 16


def low_of(word):
    return (word << 16) >> 16


def every(ref, first, stride):
    return ref[pl.ds(first, ref.shape[0] // stride, stride=stride)]


def power_of_two(k):
    return jnp.exp(k * math.log(2.0))


def scaled(x):
    most = jnp.max(jnp.abs(x), axis=1, keepdims=True)
    power = jnp.ceil(jnp.log(jnp.maximum(most, 2.0**-58)) / math.log(2.0))
    whole = jnp.clip(jnp.round(x / power_of_two(power) * FULL), -FULL, FULL)
    return whole.astype(jnp.int32), power


def in_lanes(columns, own_count):
    rows = columns[0].shape[0]
    lane = lax.broadcasted_iota(jnp.int32, (rows, LANES), 1)
    row = lax.broadcasted_iota(jnp.int32, (rows, LANES), 0)
    place = lane - (row & (own_count - 1))
    marks = jnp.zeros((rows, LANES), jnp.float32)
    for k, column in enumerate(columns):
        marks = jnp.where(place == k * own_count, column, marks)
    return jnp.sum(marks.reshape(rows // own_count, own_count, LANES), axis=1)


def in_two(x):
    high = x.astype(jnp.bfloat16)
    return high, (x - high.astype(jnp.float32)).astype(jnp.bfloat16)


def product(a, b, dims):
    def one(u, v):
        return lax.dot_general(u, v, (dims, ((), ())), preferred_element_type=jnp.float32)

    return one(a[0], b[0]) + (one(a[0], b[1]) + one(a[1], b[0]))


ROWS = ((1,), (0,))
BY_ROW = ((0,), (0,))
BY_COLUMN = ((1,), (1,))


def solve_kernel(own_count, ridge_ref, queries_ref, words_ref, high_ref, low_ref, kept_ref, system_ref, weights_ref, inverse_ref, rest_ref):
    size = system_ref.shape[0]
    inv_root = 1.0 / math.sqrt(queries_ref.shape[1])
    for k in range(own_count):
        kept_ref[pl.ds(k, size // own_count, stride=own_count)] = decoded(low_of(every(words_ref, k, own_count + 1)))
    kept = kept_ref[...].astype(jnp.bfloat16)
    logits = lax.dot_general(
        queries_ref[...], kept, (BY_COLUMN, ((), ())), preferred_element_type=jnp.float32
    ) * inv_root
    weights = jnp.exp(logits - jnp.max(logits, axis=1, keepdims=True))
    weights = weights / jnp.sum(weights, axis=1, keepdims=True)
    weights_ref[...] = weights
    parts = in_two(weights)
    gram = product(parts, parts, BY_ROW)
    ridge = jnp.max(ridge_ref[...])
    bound = jnp.max(jnp.sum(weights, axis=0, keepdims=True), axis=1, keepdims=True) * 1.0001
    row = lax.broadcasted_iota(jnp.int32, (size, size), 0)
    column = lax.broadcasted_iota(jnp.int32, (size, size), 1)
    eye = jnp.where(row == column, 1.0, 0.0)
    system = gram + ridge * eye
    system_ref[...] = system
    span = jnp.max(bound) + 2.0 * ridge
    first = 2.0 / span
    rest = eye - first * system
    rest_ref[...] = rest
    inverse_ref[...] = first * eye
    reach = span / jnp.max(bound)

    def step(reach):
        ahead = 2.0 * reach * reach
        scale = ahead / (ahead - 1.0)
        rest = in_two(rest_ref[...])
        inverse = inverse_ref[...]
        inverse_ref[...] = scale * (inverse + product(in_two(inverse), rest, ROWS))
        rest_ref[...] = scale * product(rest, rest, ROWS) - (scale - 1.0) * eye
        return ahead - 1.0

    lax.while_loop(lambda reach: reach < 4096.0, step, reach)
    inverse = inverse_ref[...]
    rest = eye - jnp.dot(
        system_ref[...], inverse, precision=lax.Precision.HIGHEST, preferred_element_type=jnp.float32
    )
    inverse = inverse + product(in_two(inverse), in_two(rest), ROWS)
    high_ref[...], low_ref[...] = in_two(product(in_two(inverse), in_two(weights_ref[...]), BY_COLUMN))


def sent_out(source, target, sems, first, rows, parts=2):
    size = rows // parts
    copies = []
    for k in range(parts):
        part = pl.ds(first + k * size, size)
        copies.append(pltpu.make_async_copy(source.at[part], target.at[part], sems.at[k]))
        copies[-1].start()
    return copies


def pick_kernel(
    level_hbm, positions_hbm, kept_hbm, keys_hbm, queries_hbm, out_hbm, ridge_hbm,
    level_ref, positions_ref, kept_ref, keys_ref, near_ref, out_ref, ridge_ref, first_sems, sems, near_sems, out_sems, ridge_sem,
):
    slab_len = keys_ref.shape[0]
    peers = out_ref.shape[0]
    own_count = positions_ref.shape[0]
    start = lax.axis_index(SEQ).astype(jnp.int32) * slab_len
    tile = near_ref.shape[0] // own_count
    rest = keys_ref.shape[0] // KEY_PARTS
    positions_copy = pltpu.make_async_copy(positions_hbm, positions_ref, first_sems.at[0])
    kept_copy = pltpu.make_async_copy(kept_hbm, kept_ref, first_sems.at[1])
    level_copy = pltpu.make_async_copy(level_hbm, level_ref, first_sems.at[2])
    positions_copy.start()
    kept_copy.start()
    level_copy.start()
    copies = []
    for k in range(KEY_PARTS):
        part = pl.ds(k * rest, rest)
        copies.append(pltpu.make_async_copy(keys_hbm.at[part], keys_ref.at[part], sems.at[k]))
        copies[-1].start()
    positions_copy.wait()
    places = [jnp.clip(positions_ref[k] - start, 0, slab_len - 1) for k in range(own_count)]
    near = []
    for k in range(own_count):
        first = pl.multiple_of((places[k] // tile) * tile, tile)
        near.append(pltpu.make_async_copy(queries_hbm.at[pl.ds(first, tile)], near_ref.at[pl.ds(k * tile, tile)], near_sems.at[k]))
        near[-1].start()
    lane = lax.broadcasted_iota(jnp.int32, (1, LANES), 1)

    def one_hot(places, size):
        return jnp.concatenate(
            [
                jnp.where(places == (lane + at).astype(jnp.float32), 1.0, 0.0).astype(jnp.bfloat16)
                for at in range(0, size, LANES)
            ],
            axis=1,
        )

    row = lax.broadcasted_iota(jnp.int32, (2 * own_count, LANES), 0)
    place = jnp.full((2 * own_count, LANES), -1, jnp.int32)
    for k in range(own_count):
        place = jnp.where(row == k, k * tile + places[k] % tile, place)
    kept_copy.wait()
    offset = (kept_ref[...] - start).astype(jnp.float32)
    offset = jnp.transpose(jnp.broadcast_to(offset, (LANES, offset.shape[1])))
    chosen = one_hot(offset, slab_len)
    level_copy.wait()
    ridge_ref[...] = jnp.full(ridge_ref.shape, level_ref[0].astype(jnp.float32) * 0.01)
    ridge_copy = pltpu.make_async_copy(ridge_ref, ridge_hbm, ridge_sem)
    ridge_copy.start()
    for copy in copies:
        copy.wait()
    picked = jnp.dot(chosen, keys_ref[...], preferred_element_type=jnp.float32)
    picked = picked.reshape(peers, -1, LANES)
    for copy in near:
        copy.wait()
    own = jnp.dot(one_hot(place.astype(jnp.float32), own_count * tile), near_ref[...], preferred_element_type=jnp.float32)
    half = peers // 2
    own = jnp.broadcast_to(own[None, :own_count], (half, own_count, LANES))
    moved = []
    for k in range(2):
        out_ref[k * half : (k + 1) * half] = jnp.concatenate([own, picked[k * half : (k + 1) * half]], axis=1).astype(jnp.bfloat16)
        moved += sent_out(out_ref, out_hbm, out_sems.at[k], k * half, half)
    ridge_copy.wait()
    for copy in moved:
        copy.wait()


def attend_kernel(own_count, got_ref, keys_ref, values_ref, queries_ref, out_ref):
    peers = got_ref.shape[0]
    rows = peers * own_count
    inv_root = 1.0 / math.sqrt(keys_ref.shape[1])
    got = got_ref[...].astype(jnp.float32)
    code = code_of(jnp.sum(got[:, own_count:], axis=0))
    queries_ref[...] = got[:, :own_count].reshape(rows, LANES).astype(jnp.bfloat16)
    block = rows // 2
    stride = own_count + 1
    for at in range(0, rows, block):
        scores = lax.dot_general(
            queries_ref[at : at + block], keys_ref[...], (BY_COLUMN, ((), ())), preferred_element_type=jnp.float32
        )
        peak = jnp.max(scores, axis=1, keepdims=True)
        probs = jnp.exp2((scores - peak) * (inv_root * math.log2(math.e))).astype(jnp.bfloat16)
        peak = peak * inv_root
        total = jnp.sum(probs.astype(jnp.float32), axis=1, keepdims=True)
        whole, power = scaled(jnp.dot(probs, values_ref[...], preferred_element_type=jnp.float32) / total)
        peak_mark = jnp.round(peak * PEAK_UNIT)
        share_mark = jnp.round((jnp.log(total) + (peak - peak_mark / PEAK_UNIT)) * SHARE_UNIT)
        marks = in_lanes((peak_mark, share_mark, power), own_count)
        count = block // own_count
        first = at // own_count * stride
        for k in range(count):
            words = packed(whole[k * own_count : (k + 1) * own_count], code)
            out_ref[first + k * stride : first + k * stride + own_count] = words
        out_ref[pl.ds(first + own_count, count, stride=stride)] = marks.astype(jnp.int32)


def merge_kernel(words_ref, ref_out_ref, out_ref):
    own_count = ref_out_ref.shape[0]
    marks = every(words_ref, own_count, own_count + 1).astype(jnp.float32)
    peaks = marks[:, :own_count] / PEAK_UNIT
    shares = marks[:, own_count : 2 * own_count] / SHARE_UNIT
    powers = marks[:, 2 * own_count : 3 * own_count]
    factors = jnp.exp(peaks - jnp.max(peaks, axis=0, keepdims=True) + shares)
    scales = factors * power_of_two(powers) * (1.0 / FULL) / jnp.sum(factors, axis=0, keepdims=True)
    ref_out = jnp.concatenate(
        [
            jnp.sum(
                high_of(every(words_ref, k, own_count + 1)).astype(jnp.float32) * scales[:, k : k + 1],
                axis=0,
                keepdims=True,
            )
            for k in range(own_count)
        ],
        axis=0,
    )
    ref_out_ref[...] = ref_out
    whole, power = scaled(ref_out)
    half = own_count // 2
    words = packed(whole[:half], whole[half:])
    words = jnp.concatenate([words, in_lanes((power,), own_count).astype(jnp.int32)], axis=0)
    peers = out_ref.shape[0] // (half + 1)
    for k in range(peers):
        out_ref[k * (half + 1) : (k + 1) * (half + 1)] = words


def finish_kernel(own_count, words_ref, high_ref, low_ref, out_hbm, out_ref, rows_ref, sems):
    half = own_count // 2
    peers = words_ref.shape[0] // (half + 1)
    scales = power_of_two(every(words_ref, half, half + 1).astype(jnp.float32)[:, :own_count]) * (1.0 / FULL)
    for k in range(own_count):
        words = every(words_ref, k % half, half + 1)
        whole = high_of(words) if k < half else low_of(words)
        rows_ref[pl.ds(k, peers, stride=own_count)] = whole.astype(jnp.float32) * scales[:, k : k + 1]
    high, low = in_two(rows_ref[...])
    both = jnp.concatenate([high, low], axis=1)
    size = out_ref.shape[0] // 2
    moved = []
    for part in range(2):
        at = part * size
        sums = jnp.dot(high_ref[at : at + size], both, preferred_element_type=jnp.float32)
        rest = jnp.dot(low_ref[at : at + size], high, preferred_element_type=jnp.float32)
        out_ref[at : at + size] = sums[:, :LANES] + (sums[:, LANES:] + rest)
        moved += sent_out(out_ref, out_hbm, sems.at[part], at, size)
    for copy in moved:
        copy.wait()


def per_device(keys, values, queries, query_positions, kept_index, ridge_level):
    slab_len, head_dim = keys.shape
    own_count = query_positions.shape[0]
    kept_count = kept_index.shape[0]
    peers = lax.axis_size(SEQ)
    own_kept = kept_count // peers
    rows = peers * own_count
    vmem = pl.BlockSpec(memory_space=pltpu.VMEM)
    hbm = pl.BlockSpec(memory_space=pltpu.HBM)
    roomy = pltpu.CompilerParams(vmem_limit_bytes=24 * 2**20)
    whole = pltpu.CompilerParams(vmem_limit_bytes=60 * 2**20)
    small = pltpu.CompilerParams(vmem_limit_bytes=8 * 2**20)
    f32, bf16, i32 = jnp.float32, jnp.bfloat16, jnp.int32
    sent, ridge = pl.pallas_call(
        pick_kernel,
        out_shape=[
            jax.ShapeDtypeStruct((peers, own_count + own_kept, head_dim), bf16),
            jax.ShapeDtypeStruct((8, LANES), f32),
        ],
        in_specs=[hbm] * 5,
        out_specs=[hbm] * 2,
        scratch_shapes=[
            pltpu.SMEM((1,), i32),
            pltpu.SMEM((own_count,), i32),
            pltpu.VMEM((1, kept_count), i32),
            pltpu.VMEM((slab_len, head_dim), bf16),
            pltpu.VMEM((own_count * TILE, head_dim), bf16),
            pltpu.VMEM((peers, own_count + own_kept, head_dim), bf16),
            pltpu.VMEM((8, LANES), f32),
            pltpu.SemaphoreType.DMA((3,)),
            pltpu.SemaphoreType.DMA((KEY_PARTS,)),
            pltpu.SemaphoreType.DMA((own_count,)),
            pltpu.SemaphoreType.DMA((2, 2)),
            pltpu.SemaphoreType.DMA,
        ],
        compiler_params=whole,
        name="pick",
    )(ridge_level, query_positions, kept_index[None], keys, queries)
    got = swap(sent)
    all_queries, words = pl.pallas_call(
        functools.partial(attend_kernel, own_count),
        out_shape=[
            jax.ShapeDtypeStruct((rows, head_dim), bf16),
            jax.ShapeDtypeStruct((peers * (own_count + 1), LANES), i32),
        ],
        in_specs=[vmem] * 3,
        out_specs=[vmem] * 2,
        compiler_params=roomy,
        name="attend",
    )(got, keys, values)
    words = swap(words.reshape(peers, own_count + 1, 1, LANES)).reshape(words.shape)
    ref_out, means = pl.pallas_call(
        merge_kernel,
        out_shape=[
            jax.ShapeDtypeStruct((own_count, head_dim), f32),
            jax.ShapeDtypeStruct((peers * (own_count // 2 + 1), LANES), i32),
        ],
        in_specs=[vmem],
        out_specs=[vmem] * 2,
        compiler_params=small,
        name="merge",
    )(words)
    means = swap(means.reshape(peers, own_count // 2 + 1, 1, LANES)).reshape(means.shape)
    square = (kept_count, kept_count)
    high, low = pl.pallas_call(
        functools.partial(solve_kernel, own_count),
        out_shape=[jax.ShapeDtypeStruct((kept_count, rows), bf16)] * 2,
        in_specs=[vmem] * 3,
        out_specs=[vmem] * 2,
        scratch_shapes=[
            pltpu.VMEM((kept_count, head_dim), f32),
            pltpu.VMEM(square, f32),
            pltpu.VMEM((rows, kept_count), f32),
            pltpu.VMEM(square, f32),
            pltpu.VMEM(square, f32),
        ],
        compiler_params=roomy,
        cost_estimate=pl.CostEstimate(flops=12 * 10**9, bytes_accessed=2 * 2**20, transcendentals=2**18),
        name="solve",
    )(ridge, all_queries, words)
    matched_values = pl.pallas_call(
        functools.partial(finish_kernel, own_count),
        out_shape=jax.ShapeDtypeStruct((kept_count, head_dim), f32),
        in_specs=[vmem] * 3,
        out_specs=hbm,
        scratch_shapes=[
            pltpu.VMEM((kept_count, head_dim), f32),
            pltpu.VMEM((rows, head_dim), f32),
            pltpu.SemaphoreType.DMA((2, 2)),
        ],
        compiler_params=roomy,
        name="finish",
    )(means, high, low)
    return (matched_values, ref_out)


def solution(mesh):
    return jax.shard_map(
        per_device,
        mesh=mesh,
        in_specs=(
            P(("head", "seq"), None),
            P(("head", "seq"), None),
            P(("head", "seq"), None),
            P(("head", "seq")),
            P("head"),
            P("head"),
        ),
        out_specs=(P("head", None), P(("head", "seq"), None)),
        check_vma=False,
    )
```
